32 devices in a mesh: row: 4 (over y, x), col: 8 (over z, core).
Axes of the slice: x: 2, y: 2, z: 4, core: 2. Of those that a mesh axis runs over, the one named last changes fastest.
Arguments:
- filtered_bands: bfloat16 [4096, 16384], P(None, ('row', 'col')), may hold values from -0.09375 to 0.09375
Outputs:
- gram_upper: float32 [16384, 16384], P('row', 'col')
The draws below stay inside these ranges and needn't reach their ends.
All inputs are finite; a program needn't handle non-finite values.
Results may differ from the reference program's by a relative error of at most 0.0003.
Values may be sent and summed in bfloat16 or wider, within the bound.
A program may use at most 192 MiB of HBM per device.

```python
import jax
import jax.numpy as jnp
from jax import lax

NB = 16384
G = 4096


def block_scale(own_key, shape, cuts, smallest, top_value):
    loudness = 1.0
    for axis_at, blocks in cuts:
        draws = jax.random.uniform(jax.random.fold_in(jax.random.fold_in(own_key, 6), axis_at), (blocks,), jnp.float32, smallest / len(cuts), top_value / len(cuts))
        loudness = loudness * jnp.repeat(jnp.exp(draws), shape[axis_at] // blocks).reshape((-1,) + (1,) * (len(shape) - 1 - axis_at))
    return loudness


def normal_values(rng, shape, scale, reach, cuts=(), dtype=jnp.bfloat16):
    loudness = block_scale(rng, shape, cuts, -0.22, 0.18) if cuts else 1.0
    array = jax.random.normal(rng, shape, jnp.float32) * scale * loudness
    return jnp.minimum(jnp.maximum(array, -reach), reach).astype(dtype)


def setup_inputs(seed: int = 0) -> dict:
    seeds = jax.random.split(jax.random.key(seed), 2)
    filtered_bands = normal_values(seeds[0], (G, NB), G ** -0.5, 0.09375, ((1, 32),))
    return dict(filtered_bands=filtered_bands)


def reference(filtered_bands):
    widened = filtered_bands.astype(jnp.float32)
    correlation = lax.dot_general(widened, widened, (((0,), (0,)), ((), ())), precision=lax.Precision.HIGHEST, preferred_element_type=jnp.float32)
    return jnp.triu(correlation)
```

```python
import functools

import jax
import jax.numpy as jnp
from jax import lax
from jax.experimental import pallas as pl
from jax.experimental.pallas import tpu as pltpu
from jax.sharding import PartitionSpec as P

MESH = pl.DeviceIdType.MESH
CHUNKS = 8
AHEAD = 2
VMEM_BYTES = 56 * 2**20


def ring_place(row, count):
    return jnp.where(row % 2 == 0, row // 2, count - 1 - row // 2)


def ring_row(place, count):
    return jnp.where(place < count // 2, 2 * place, 2 * (count - 1 - place) + 1)


def hops_needed(count, group, direction):
    place = lambda row: row // 2 if row % 2 == 0 else count - 1 - row // 2
    steps = [(direction * (place(row) - place(group))) % count for row in range(group)]
    return max(steps, default=0)


def gather_kernel(
    row_count, col_count, own_ref, rows_ref, cols_ref, part_ref,
    rows_v, cols_v, total,
    row_recv, sib_recv, col_recv, up_send, down_send, sib_send, col_send, local, load,
):
    chips = col_count // 2
    depth, bands = own_ref.shape
    piece = depth // CHUNKS
    row = lax.axis_index("row")
    col = lax.axis_index("col")
    chip, core = col // 2, col % 2
    wanted = chip >= row
    diagonal = chip == row

    upper = (row, col + 2)
    lower = (row, col - 2)
    sibling = (row, chip * 2 + 1 - core)
    forward = core == 0
    here, start = ring_place(row, row_count), ring_place(chip, row_count)
    after, before = (here + 1) % row_count, (here + row_count - 1) % row_count
    row_after, row_before = ring_row(after, row_count), ring_row(before, row_count)
    hop = jnp.where(
        forward, (here - start + row_count) % row_count, (start - here + row_count) % row_count
    )
    hops = jnp.int32(0)
    for group in range(row_count):
        fixed = jnp.where(
            forward, hops_needed(row_count, group, 1), hops_needed(row_count, group, -1)
        )
        hops = jnp.where(chip == group, fixed, hops)
    next_on_ring = (jnp.where(forward, row_after, row_before), col)
    takes_cols = (hop >= 1) & (hop <= hops)
    gives_cols = hop < hops

    barrier = pltpu.get_barrier_semaphore()

    def greet(device):
        pl.semaphore_signal(barrier, inc=1, device_id=device, device_id_type=MESH)

    has_upper, has_lower = chip < chips - 1, chip > 0
    pl.when(has_upper)(lambda: greet(upper))
    pl.when(has_lower)(lambda: greet(lower))
    greet(sibling)
    greet((row_after, col))
    greet((row_before, col))
    pl.semaphore_wait(barrier, 3 + has_upper.astype(jnp.int32) + has_lower.astype(jnp.int32))

    def part(j):
        return pl.ds(pl.multiple_of(j * piece, piece), piece)

    def block_copy(source, chip_at, j, send, recv, device):
        block = chip_at * 2 + core
        return pltpu.make_async_remote_copy(
            src_ref=own_ref.at[part(j)] if source == "own" else rows_ref.at[block, part(j)],
            dst_ref=rows_ref.at[block, part(j)],
            send_sem=send.at[chip_at, j],
            recv_sem=recv.at[chip_at, j],
            device_id=device,
            device_id_type=MESH,
        )

    def up(source, chip_at, j):
        return block_copy(source, chip_at, j, up_send, row_recv, upper)

    def down(source, chip_at, j):
        return block_copy(source, chip_at, j, down_send, row_recv, lower)

    def across(source, chip_at, j):
        return block_copy(source, chip_at, j, sib_send, sib_recv, sibling)

    def col_copy(from_rows, i, j):
        return pltpu.make_async_remote_copy(
            src_ref=rows_ref.at[core * row_count + i, part(j)]
            if from_rows
            else cols_ref.at[i, part(j)],
            dst_ref=cols_ref.at[i, part(j)],
            send_sem=col_send.at[i, j],
            recv_sem=col_recv.at[i, j],
            device_id=next_on_ring,
            device_id_type=MESH,
        )

    sends_down = has_lower & (chip - 1 >= row)

    def send_own(j):
        pl.when(has_upper)(lambda: up("own", chip, j).start())
        pl.when(sends_down)(lambda: down("own", chip, j).start())
        pl.when(wanted)(lambda: across("own", chip, j).start())

    for j in range(AHEAD):
        send_own(j)
    own_copy = pltpu.make_async_copy(own_ref, rows_ref.at[col], local.at[0])
    own_copy.start()

    @pl.when(wanted)
    def _():
        @pl.loop(0, total.shape[0] // bands)
        def _(rb):
            at = pl.ds(pl.multiple_of(rb * bands, bands), bands)
            total[at, :] = jnp.zeros((bands, total.shape[1]), jnp.float32)

    own_copy.wait()

    def multiply(j):
        rows_load = pltpu.make_async_copy(rows_ref.at[:, part(j)], rows_v, load.at[0])
        cols_load = pltpu.make_async_copy(cols_ref.at[:, part(j)], cols_v, load.at[1])
        rows_load.start()
        cols_load.start()
        rows_load.wait()
        cols_load.wait()

        @pl.loop(0, col_count)
        def _(rb):
            lhs = rows_v[rb].T
            at = pl.ds(pl.multiple_of(rb * bands, bands), bands)
            for cb in range(row_count):

                @pl.when(jnp.logical_not(diagonal) | (core * row_count + cb >= rb))
                def _():
                    there = pl.ds(cb * bands, bands)
                    total[at, there] += jnp.dot(
                        lhs, cols_v[cb], preferred_element_type=jnp.float32
                    )

    def save():
        return pltpu.make_async_copy(total, part_ref, load.at[2])

    @pl.loop(0, CHUNKS)
    def _(j):
        pl.when(j + AHEAD < CHUNKS)(lambda: send_own(j + AHEAD))
        for d in range(1, chips):

            @pl.when(chip >= d)
            def _():
                at = chip - d
                up("rows", at, j).wait_recv()
                pl.when(has_upper)(lambda: up("rows", at, j).start())
                pl.when(wanted)(lambda: across("rows", at, j).start())

        for d in range(1, chips):

            @pl.when(wanted & (chip + d < chips))
            def _():
                at = chip + d
                down("rows", at, j).wait_recv()
                pl.when(sends_down)(lambda: down("rows", at, j).start())
                across("rows", at, j).start()

        @pl.when(takes_cols)
        def _():
            for i in range(row_count):
                col_copy(False, i, j).wait_recv()
                pl.when(gives_cols)(lambda: col_copy(False, i, j).start())

        @pl.when(wanted)
        def _():
            for at in range(chips):
                other = at * 2 + 1 - core
                pltpu.make_async_remote_copy(
                    src_ref=rows_ref.at[other, part(j)],
                    dst_ref=rows_ref.at[other, part(j)],
                    send_sem=sib_send.at[at, j],
                    recv_sem=sib_recv.at[at, j],
                    device_id=sibling,
                    device_id_type=MESH,
                ).wait_recv()

        @pl.when(diagonal)
        def _():
            for i in range(row_count):
                pl.when(gives_cols)(lambda: col_copy(True, i, j).start())
            mine = pltpu.make_async_copy(
                rows_ref.at[pl.ds(core * row_count, row_count), part(j)],
                cols_ref.at[:, part(j)],
                local.at[1],
            )
            mine.start()
            mine.wait()

        @pl.when(wanted & (j < CHUNKS - 1))
        def _():
            multiply(j)
            pl.when(j == CHUNKS - 2)(lambda: save().start())

    @pl.loop(0, CHUNKS)
    def _(j):
        for at in range(chips):
            pl.when(has_upper & (chip >= at))(lambda: up("rows", at, j).wait_send())
            pl.when(sends_down & (chip <= at))(lambda: down("rows", at, j).wait_send())
            pl.when(wanted)(lambda: across("rows", at, j).wait_send())
        for i in range(row_count):
            pl.when(gives_cols)(lambda: col_copy(False, i, j).wait_send())

    pl.when(wanted)(lambda: save().wait())


def finish_kernel(rows_ref, cols_ref, part_ref, out_ref):
    bands = rows_ref.shape[2]
    tile_cols = out_ref.shape[1]
    row = lax.axis_index("row")
    col = lax.axis_index("col")
    rb = pl.program_id(0)
    first_row = (row * pl.num_programs(0) + rb) * bands
    first_col = col * tile_cols
    needed = first_col + tile_cols > first_row

    @pl.when(needed)
    def _():
        lhs = rows_ref[0].T
        for cb in range(tile_cols // bands):
            at = pl.ds(cb * bands, bands)
            value = part_ref[:, at] + jnp.dot(
                lhs, cols_ref[cb], preferred_element_type=jnp.float32
            )
            global_rows = first_row + lax.broadcasted_iota(jnp.int32, (bands, bands), 0)
            global_cols = (
                first_col + cb * bands + lax.broadcasted_iota(jnp.int32, (bands, bands), 1)
            )
            out_ref[:, at] = jnp.where(global_cols >= global_rows, value, 0.0)

    @pl.when(jnp.logical_not(needed))
    def _():
        out_ref[...] = jnp.zeros_like(out_ref)


def shards(row_count, col_count, own):
    depth, bands = own.shape
    tile_rows, tile_cols = bands * col_count, bands * row_count
    piece = depth // CHUNKS
    chips = col_count // 2
    hbm = pl.BlockSpec(memory_space=pl.ANY)
    flops = 2 * tile_rows * tile_cols * depth
    dma = lambda first: pltpu.SemaphoreType.DMA((first, CHUNKS))
    rows, cols, part = pl.pallas_call(
        functools.partial(gather_kernel, row_count, col_count),
        out_shape=(
            jax.ShapeDtypeStruct((col_count, depth, bands), own.dtype),
            jax.ShapeDtypeStruct((row_count, depth, bands), own.dtype),
            jax.ShapeDtypeStruct((tile_rows, tile_cols), jnp.float32),
        ),
        in_specs=[hbm],
        out_specs=(hbm, hbm, hbm),
        scratch_shapes=[
            pltpu.VMEM((col_count, piece, bands), own.dtype),
            pltpu.VMEM((row_count, piece, bands), own.dtype),
            pltpu.VMEM((tile_rows, tile_cols), jnp.float32),
            dma(chips), dma(chips), dma(row_count),
            dma(chips), dma(chips), dma(chips), dma(row_count),
            pltpu.SemaphoreType.DMA((2,)),
            pltpu.SemaphoreType.DMA((3,)),
        ],
        compiler_params=pltpu.CompilerParams(
            collective_id=0, has_side_effects=True, vmem_limit_bytes=VMEM_BYTES
        ),
        cost_estimate=pl.CostEstimate(
            flops=flops * (CHUNKS - 1) // CHUNKS,
            bytes_accessed=(tile_rows + tile_cols) * (2 * depth + 2 * tile_cols),
            transcendentals=0,
        ),
        name="gather",
    )(own)
    return pl.pallas_call(
        finish_kernel,
        grid=(col_count,),
        out_shape=jax.ShapeDtypeStruct((tile_rows, tile_cols), jnp.float32),
        in_specs=[
            pl.BlockSpec((1, piece, bands), lambda rb: (rb, CHUNKS - 1, 0)),
            pl.BlockSpec((row_count, piece, bands), lambda rb: (0, CHUNKS - 1, 0)),
            pl.BlockSpec((bands, tile_cols), lambda rb: (rb, 0)),
        ],
        out_specs=pl.BlockSpec((bands, tile_cols), lambda rb: (rb, 0)),
        compiler_params=pltpu.CompilerParams(vmem_limit_bytes=VMEM_BYTES),
        cost_estimate=pl.CostEstimate(
            flops=flops // CHUNKS,
            bytes_accessed=8 * tile_rows * tile_cols,
            transcendentals=0,
        ),
        name="finish",
    )(rows, cols, part)


def solution(mesh):
    return jax.shard_map(
        functools.partial(shards, mesh.shape["row"], mesh.shape["col"]),
        mesh=mesh,
        in_specs=(P(None, ("row", "col")),),
        out_specs=P("row", "col"),
        check_vma=False,
    )
```

```python
import functools

import jax
import jax.numpy as jnp
from jax import lax
from jax.experimental import pallas as pl
from jax.experimental.pallas import tpu as pltpu
from jax.sharding import PartitionSpec as P

MESH = pl.DeviceIdType.MESH
CHUNKS = 8
AHEAD = 1
VMEM_BYTES = 56 * 2**20


def ring_place(row, count):
    return jnp.where(row % 2 == 0, row // 2, count - 1 - row // 2)


def ring_row(place, count):
    return jnp.where(place < count // 2, 2 * place, 2 * (count - 1 - place) + 1)


def hops_needed(count, group, direction):
    place = lambda row: row // 2 if row % 2 == 0 else count - 1 - row // 2
    steps = [(direction * (place(row) - place(group))) % count for row in range(group)]
    return max(steps, default=0)


def gather_kernel(
    row_count, col_count, own_ref, rows_ref, cols_ref, part_ref,
    rows_v, cols_v, total,
    row_recv, sib_recv, col_recv, up_send, down_send, sib_send, col_send, local, load, saved,
):
    chips = col_count // 2
    depth, bands = own_ref.shape
    piece = depth // CHUNKS
    row = lax.axis_index("row")
    col = lax.axis_index("col")
    chip, core = col // 2, col % 2
    wanted = chip >= row
    diagonal = chip == row

    upper = (row, col + 2)
    lower = (row, col - 2)
    sibling = (row, chip * 2 + 1 - core)
    forward = core == 0
    here, start = ring_place(row, row_count), ring_place(chip, row_count)
    after, before = (here + 1) % row_count, (here + row_count - 1) % row_count
    row_after, row_before = ring_row(after, row_count), ring_row(before, row_count)
    hop = jnp.where(
        forward, (here - start + row_count) % row_count, (start - here + row_count) % row_count
    )
    hops = jnp.int32(0)
    for group in range(row_count):
        fixed = jnp.where(
            forward, hops_needed(row_count, group, 1), hops_needed(row_count, group, -1)
        )
        hops = jnp.where(chip == group, fixed, hops)
    next_on_ring = (jnp.where(forward, row_after, row_before), col)
    takes_cols = (hop >= 1) & (hop <= hops)
    gives_cols = hop < hops

    barrier = pltpu.get_barrier_semaphore()

    def greet(device):
        pl.semaphore_signal(barrier, inc=1, device_id=device, device_id_type=MESH)

    has_upper, has_lower = chip < chips - 1, chip > 0
    pl.when(has_upper)(lambda: greet(upper))
    pl.when(has_lower)(lambda: greet(lower))
    greet(sibling)
    greet((row_after, col))
    greet((row_before, col))
    pl.semaphore_wait(barrier, 3 + has_upper.astype(jnp.int32) + has_lower.astype(jnp.int32))

    def part(j):
        return pl.ds(pl.multiple_of(j * piece, piece), piece)

    def block_copy(source, chip_at, j, send, recv, device):
        block = chip_at * 2 + core
        return pltpu.make_async_remote_copy(
            src_ref=own_ref.at[part(j)] if source == "own" else rows_ref.at[block, part(j)],
            dst_ref=rows_ref.at[block, part(j)],
            send_sem=send.at[chip_at, j],
            recv_sem=recv.at[chip_at, j],
            device_id=device,
            device_id_type=MESH,
        )

    def up(source, chip_at, j):
        return block_copy(source, chip_at, j, up_send, row_recv, upper)

    def down(source, chip_at, j):
        return block_copy(source, chip_at, j, down_send, row_recv, lower)

    def across(source, chip_at, j):
        return block_copy(source, chip_at, j, sib_send, sib_recv, sibling)

    def col_copy(from_rows, i, j):
        return pltpu.make_async_remote_copy(
            src_ref=rows_ref.at[core * row_count + i, part(j)]
            if from_rows
            else cols_ref.at[i, part(j)],
            dst_ref=cols_ref.at[i, part(j)],
            send_sem=col_send.at[i, j],
            recv_sem=col_recv.at[i, j],
            device_id=next_on_ring,
            device_id_type=MESH,
        )

    sends_down = has_lower & (chip - 1 >= row)

    def send_own(j):
        pl.when(has_upper)(lambda: up("own", chip, j).start())
        pl.when(sends_down)(lambda: down("own", chip, j).start())
        pl.when(wanted)(lambda: across("own", chip, j).start())

    for j in range(AHEAD):
        send_own(j)

    def own_in(j):
        return pltpu.make_async_copy(
            own_ref.at[part(j)], rows_v.at[0, j % col_count], local.at[0, j]
        )

    def own_out(j):
        return pltpu.make_async_copy(
            rows_v.at[0, j % col_count], rows_ref.at[col, part(j)], local.at[1, j]
        )

    @pl.when(wanted)
    def _():
        for first in range(0, CHUNKS, col_count):
            batch = range(first, min(first + col_count, CHUNKS))
            for j in batch:
                own_in(j).start()
            for j in batch:
                own_in(j).wait()
                own_out(j).start()
            for j in batch:
                own_out(j).wait()

        @pl.loop(0, total.shape[0] // bands)
        def _(rb):
            at = pl.ds(pl.multiple_of(rb * bands, bands), bands)
            total[at, :] = jnp.zeros((bands, total.shape[1]), jnp.float32)

    same_rows = pl.ds(core * row_count, row_count)

    def load_rows(j):
        return pltpu.make_async_copy(
            rows_ref.at[:, part(j)], rows_v.at[j % 2], load.at[0, j % 2]
        )

    def load_cols(j, same):
        source = rows_ref.at[same_rows, part(j)] if same else cols_ref.at[:, part(j)]
        return pltpu.make_async_copy(source, cols_v.at[j % 2], load.at[1, j % 2])

    def fetch(j):
        load_rows(j).start()
        pl.when(diagonal)(lambda: load_cols(j, True).start())
        pl.when(jnp.logical_not(diagonal))(lambda: load_cols(j, False).start())

    def multiply(j):
        load_rows(j).wait()
        load_cols(j, False).wait()

        @pl.loop(0, col_count)
        def _(rb):
            lhs = rows_v[j % 2, rb].T
            at = pl.ds(pl.multiple_of(rb * bands, bands), bands)
            for cb in range(row_count):

                @pl.when(jnp.logical_not(diagonal) | (core * row_count + cb >= rb))
                def _():
                    there = pl.ds(cb * bands, bands)
                    total[at, there] += jnp.dot(
                        lhs, cols_v[j % 2, cb], preferred_element_type=jnp.float32
                    )

    def save():
        return pltpu.make_async_copy(total, part_ref, saved)

    def sibling_arrived(j):
        for at in range(chips):
            other = at * 2 + 1 - core
            pltpu.make_async_remote_copy(
                src_ref=rows_ref.at[other, part(j)],
                dst_ref=rows_ref.at[other, part(j)],
                send_sem=sib_send.at[at, j],
                recv_sem=sib_recv.at[at, j],
                device_id=sibling,
                device_id_type=MESH,
            ).wait_recv()

    def pass_rows(j):
        pl.when(j + AHEAD < CHUNKS)(lambda: send_own(j + AHEAD))
        for d in range(1, chips):

            @pl.when(chip >= d)
            def _():
                at = chip - d
                up("rows", at, j).wait_recv()
                pl.when(has_upper)(lambda: up("rows", at, j).start())
                pl.when(wanted)(lambda: across("rows", at, j).start())

        for d in range(1, chips):

            @pl.when(wanted & (chip + d < chips))
            def _():
                at = chip + d
                down("rows", at, j).wait_recv()
                pl.when(sends_down)(lambda: down("rows", at, j).start())
                across("rows", at, j).start()

        @pl.when(diagonal)
        def _():
            sibling_arrived(j)
            for i in range(row_count):
                pl.when(gives_cols)(lambda: col_copy(True, i, j).start())

    def pass_cols(j):
        @pl.when(takes_cols)
        def _():
            for i in range(row_count):
                col_copy(False, i, j).wait_recv()
                pl.when(gives_cols)(lambda: col_copy(False, i, j).start())

    @pl.loop(0, CHUNKS)
    def _(j):
        pass_rows(j)

        @pl.when(j >= 1)
        def _():
            pass_cols(j - 1)
            pl.when(wanted & jnp.logical_not(diagonal))(lambda: sibling_arrived(j - 1))

            @pl.when(wanted)
            def _():
                fetch(j - 1)
                pl.when(j >= 2)(lambda: multiply(j - 2))

    pl.when(gives_cols)(lambda: pass_cols(CHUNKS - 1))

    @pl.when(wanted)
    def _():
        multiply(CHUNKS - 2)
        save().start()

    pl.when(jnp.logical_not(gives_cols))(lambda: pass_cols(CHUNKS - 1))
    pl.when(wanted & jnp.logical_not(diagonal))(lambda: sibling_arrived(CHUNKS - 1))

    @pl.when(diagonal)
    def _():
        load_cols(CHUNKS - 1, True).start()
        load_cols(CHUNKS - 1, True).wait()
        mine = pltpu.make_async_copy(
            cols_v.at[(CHUNKS - 1) % 2], cols_ref.at[:, part(CHUNKS - 1)], load.at[1, 0]
        )
        mine.start()
        mine.wait()

    @pl.loop(0, CHUNKS)
    def _(j):
        for at in range(chips):
            pl.when(has_upper & (chip >= at))(lambda: up("rows", at, j).wait_send())
            pl.when(sends_down & (chip <= at))(lambda: down("rows", at, j).wait_send())
            pl.when(wanted)(lambda: across("rows", at, j).wait_send())
        for i in range(row_count):
            pl.when(gives_cols)(lambda: col_copy(False, i, j).wait_send())

    pl.when(wanted)(lambda: save().wait())


def finish_kernel(rows_ref, cols_ref, part_ref, out_ref):
    bands = rows_ref.shape[2]
    tile_cols = out_ref.shape[1]
    row = lax.axis_index("row")
    col = lax.axis_index("col")
    rb = pl.program_id(0)
    first_row = (row * pl.num_programs(0) + rb) * bands
    first_col = col * tile_cols
    needed = first_col + tile_cols > first_row

    @pl.when(needed)
    def _():
        lhs = rows_ref[0].T
        for cb in range(tile_cols // bands):
            at = pl.ds(cb * bands, bands)
            value = part_ref[:, at] + jnp.dot(
                lhs, cols_ref[cb], preferred_element_type=jnp.float32
            )
            global_rows = first_row + lax.broadcasted_iota(jnp.int32, (bands, bands), 0)
            global_cols = (
                first_col + cb * bands + lax.broadcasted_iota(jnp.int32, (bands, bands), 1)
            )
            out_ref[:, at] = jnp.where(global_cols >= global_rows, value, 0.0)

    @pl.when(jnp.logical_not(needed))
    def _():
        out_ref[...] = jnp.zeros_like(out_ref)


def shards(row_count, col_count, own):
    depth, bands = own.shape
    tile_rows, tile_cols = bands * col_count, bands * row_count
    piece = depth // CHUNKS
    chips = col_count // 2
    hbm = pl.BlockSpec(memory_space=pl.ANY)
    flops = 2 * tile_rows * tile_cols * depth
    dma = lambda first: pltpu.SemaphoreType.DMA((first, CHUNKS))
    rows, cols, part = pl.pallas_call(
        functools.partial(gather_kernel, row_count, col_count),
        out_shape=(
            jax.ShapeDtypeStruct((col_count, depth, bands), own.dtype),
            jax.ShapeDtypeStruct((row_count, depth, bands), own.dtype),
            jax.ShapeDtypeStruct((tile_rows, tile_cols), jnp.float32),
        ),
        in_specs=[hbm],
        out_specs=(hbm, hbm, hbm),
        scratch_shapes=[
            pltpu.VMEM((2, col_count, piece, bands), own.dtype),
            pltpu.VMEM((2, row_count, piece, bands), own.dtype),
            pltpu.VMEM((tile_rows, tile_cols), jnp.float32),
            dma(chips), dma(chips), dma(row_count),
            dma(chips), dma(chips), dma(chips), dma(row_count),
            dma(2),
            pltpu.SemaphoreType.DMA((2, 2)),
            pltpu.SemaphoreType.DMA,
        ],
        compiler_params=pltpu.CompilerParams(
            collective_id=0, has_side_effects=True, vmem_limit_bytes=VMEM_BYTES
        ),
        cost_estimate=pl.CostEstimate(
            flops=flops * (CHUNKS - 1) // CHUNKS,
            bytes_accessed=(tile_rows + tile_cols) * (2 * depth + 2 * tile_cols),
            transcendentals=0,
        ),
        name="gather",
    )(own)
    return pl.pallas_call(
        finish_kernel,
        grid=(col_count,),
        out_shape=jax.ShapeDtypeStruct((tile_rows, tile_cols), jnp.float32),
        in_specs=[
            pl.BlockSpec((1, piece, bands), lambda rb: (rb, CHUNKS - 1, 0)),
            pl.BlockSpec((row_count, piece, bands), lambda rb: (0, CHUNKS - 1, 0)),
            pl.BlockSpec((bands, tile_cols), lambda rb: (rb, 0)),
        ],
        out_specs=pl.BlockSpec((bands, tile_cols), lambda rb: (rb, 0)),
        compiler_params=pltpu.CompilerParams(vmem_limit_bytes=VMEM_BYTES),
        cost_estimate=pl.CostEstimate(
            flops=flops // CHUNKS,
            bytes_accessed=8 * tile_rows * tile_cols,
            transcendentals=0,
        ),
        name="finish",
    )(rows, cols, part)


def solution(mesh):
    return jax.shard_map(
        functools.partial(shards, mesh.shape["row"], mesh.shape["col"]),
        mesh=mesh,
        in_specs=(P(None, ("row", "col")),),
        out_specs=P("row", "col"),
        check_vma=False,
    )
```
